512 devices in a mesh: row: 16 (over x, y_hi), col: 32 (over y_lo, z, core).
Axes of the slice: x: 4, y: 8 (y_hi: 4, y_lo: 2; y = y_hi * 2 + y_lo), z: 8, core: 2. Of those that a mesh axis runs over, the one named last changes fastest.
Arguments:
- phase: float32 [6, 262144], P(None, ('row', 'col')), may hold values from -6 to 6
- masses: float32 [1, 262144], P(None, ('row', 'col')), may hold values from 0.1 to 10
- active_index: int32 [8192], P('col'), may hold values from 0 to 262143, as said below
Outputs:
- accel: float32 [3, 8192], P(None, 'col')
- jerk: float32 [3, 8192], P(None, 'col')
The draws below stay inside these ranges and needn't reach their ends.
Inputs may be any that keep to these rules, and one draw needn't show every extreme that they name: `active_index`: distinct star indices; 0 and 262143 are always among them.
All inputs are finite; a program needn't handle non-finite values.
Results may differ from the reference program's by a relative error of at most 0.0003.
Values sent between devices are 32-bit elements; how exact they have to be, the bound alone decides.
No kernel may reach another device: no remote copies, remote signals or barrier semaphores. Data moves between devices by JAX's collectives and lax.ppermute only.
A program may use at most 64 MiB of HBM per device.

```python
import math
import jax
import jax.numpy as jnp
from jax import lax

NSTARS = 262144
ACT = 8192


def draw_active_index(key, part):
    key = jax.random.fold_in(key, 7)
    first_key, second_key = jax.random.split(key)
    chosen = jax.random.permutation(first_key, NSTARS - 2)[:ACT - 2] + 1
    combined = jnp.concatenate([jnp.array([0, NSTARS - 1], jnp.int32), chosen.astype(jnp.int32)])
    return jax.random.permutation(second_key, combined).astype(jnp.int32)


def shard_levels(key, extent, pieces, low, high):
    gain, own = 1.0, jax.random.fold_in(key, 6)
    for position, blocks in pieces:
        draws = jnp.exp(jax.random.uniform(jax.random.fold_in(own, position), (blocks,), jnp.float32, low / len(pieces), high / len(pieces)))
        gain = gain * jnp.repeat(draws, extent[position] // blocks).reshape([-1 if axis == position else 1 for axis in range(len(extent))])
    return gain


def normal_values(key, shape, scale, limit, cuts=(), dtype=jnp.bfloat16):
    values = jax.random.normal(key, shape, jnp.float32) * scale
    if len(cuts) > 0:
        values = shard_levels(key, shape, cuts, -0.22, 0.18) * values
    return jnp.clip(values, min=-limit, max=limit).astype(dtype)


def setup_inputs(seed: int = 0) -> dict:
    key_list = jax.random.split(jax.random.key(seed), 4)
    return {
        "phase": normal_values(key_list[0], (6, NSTARS), 1.0, 6.0, ((1, 512),), jnp.float32),
        "masses": jnp.clip(jnp.exp(math.log(10.0) - 4.6051702 * jax.random.uniform(key_list[1], (1, NSTARS), jnp.float32) ** shard_levels(key_list[1], (1, NSTARS), ((1, 512),), -0.2, 0.2)), 0.1, 10.0),
        "active_index": draw_active_index(jax.random.fold_in(key_list[3], 71), 0),
    }


SOFTEN_SQ = 0.0001

def pair_terms(active_state, field_block):
    offset = field_block[0:3, None, :] - active_state[0:3, :, None]
    relative = field_block[3:6, None, :] - active_state[3:6, :, None]
    distance_sq = lax.optimization_barrier(jnp.sum(offset * offset, axis=0)) + SOFTEN_SQ
    inverse = lax.rsqrt(distance_sq)
    weight = field_block[6][None, :] * inverse * inverse * inverse
    radial_rate = 3.0 * lax.optimization_barrier(jnp.sum(offset * relative, axis=0)) / distance_sq
    accel_sum = lax.optimization_barrier(jnp.sum(weight[None] * offset, axis=2))
    jerk_sum = lax.optimization_barrier(jnp.sum(weight[None] * (relative - radial_rate[None] * offset), axis=2))
    return jnp.concatenate([accel_sum, jerk_sum], axis=0)

def reference(phase, masses, active_index):
    active_state = jnp.take(phase, active_index.astype(jnp.int32), axis=1)
    field = jnp.concatenate([phase, masses], axis=0)
    width = min(NSTARS, 1024)
    stacked = jnp.transpose(field.reshape(7, NSTARS // width, width), (1, 0, 2))

    def add_block(running, field_block):
        return (running + pair_terms(active_state, field_block), None)
    running, _ = lax.scan(add_block, jnp.zeros((6, ACT), jnp.float32), stacked)
    running = running * (1.0 / NSTARS)
    return (running[0:3], running[3:6])
```

```python
import functools

import jax
import jax.numpy as jnp
from jax import lax
from jax.experimental import pallas as pl
from jax.experimental.pallas import tpu as pltpu
from jax.sharding import Mesh, PartitionSpec as P

SOFTEN_SQ = 0.0001
NAMES = ("x", "yh", "yl", "z", "c")
ROW = ("x", "yh")
COL = ("yl", "z", "c")
LANES = 128
F32 = jnp.float32
BF16 = jnp.bfloat16


def pieces(value):
    high = value.astype(BF16)
    rest = value - high.astype(F32)
    middle = rest.astype(BF16)
    low = (rest - middle.astype(F32)).astype(BF16)
    return high, middle, low


def pick_kernel(slab_ref, place_ref, out_ref):
    blocks, _, width = slab_ref.shape
    count = place_ref.shape[1]
    block = place_ref[0:1, :]
    place = place_ref[1:2, :]
    one_hot = lax.broadcasted_iota(jnp.int32, (blocks, count), 0) == block
    one_hot = jnp.where(one_hot, 1.0, 0.0).astype(BF16)
    one_hot = jnp.concatenate([one_hot, one_hot, one_hot], axis=0)
    here = lax.broadcasted_iota(jnp.int32, (width, count), 0) == place
    rows = []
    for c in range(6):
        values = jnp.concatenate(pieces(slab_ref[:, c, :]), axis=0)
        taken = lax.dot_general(
            values, one_hot, (((0,), (0,)), ((), ())), preferred_element_type=F32
        )
        rows.append(jnp.sum(jnp.where(here, taken, 0.0), axis=0, keepdims=True))
    rows.append(jnp.zeros((2, count), F32))
    out_ref[...] = jnp.concatenate(rows, axis=0)


def field_kernel(slab_ref, sums_ref, dots_ref, centre_ref):
    blocks, _, width = slab_ref.shape
    total = jnp.zeros((8, width), F32)
    for b in range(blocks):
        total = total + slab_ref[b]
    row = lax.broadcasted_iota(jnp.int32, (8, 1), 0)
    mean = jnp.sum(total, axis=1, keepdims=True) * (1.0 / (blocks * width))
    centre = jnp.where(row < 6, mean, 0.0)
    centre_ref[...] = jnp.broadcast_to(centre, (8, LANES))
    rows = lax.broadcasted_iota(jnp.int32, (8, width), 0)
    for b in range(blocks):
        where = slice(b * width, (b + 1) * width)
        star = slab_ref[b] - centre
        mass = star[6:7, :]
        high, middle, low = pieces(jnp.where(rows == 6, mass, star * mass))
        sums_ref[:, where] = jnp.concatenate([high, middle, low, jnp.zeros_like(low)], axis=0)
        along = jnp.sum(star[0:3, :] * star[3:6, :], axis=0, keepdims=True)
        terms = jnp.where(rows == 6, along, star)
        terms = jnp.where(rows == 7, 1.0, terms)
        high, middle, low = pieces(terms)
        dots_ref[:, where] = jnp.concatenate([high, high, middle, middle, high, low], axis=0)


def pair_kernel(slab_ref, sums_ref, dots_ref, centre_ref, picks_ref, out_ref,
                spread, left, dot, terms, total, *, width, rows, lanes):
    count = picks_ref.shape[2]
    blocks, _, block_width = slab_ref.shape
    state = picks_ref[0]
    for p in range(1, picks_ref.shape[0]):
        state = state + picks_ref[p]
    columns = jnp.transpose(state)
    for c in range(3):
        spread[c] = jnp.broadcast_to(columns[:, c:c + 1], (count, LANES))
    local = state - centre_ref[:, 0:1]
    position, velocity = local[0:3, :], local[3:6, :]
    along = jnp.sum(position * velocity, axis=0, keepdims=True)
    ones = jnp.ones((1, count), F32)
    against = jnp.concatenate([-velocity, -position, ones, along], axis=0)
    high, middle, low = pieces(against)
    stack = [high, middle, high, middle, low, high]
    stack = jnp.concatenate([part.astype(F32) for part in stack], axis=0)
    left[...] = jnp.transpose(stack).astype(BF16)
    total[...] = jnp.zeros_like(total)

    def step(j, _):
        chunk = pl.ds(pl.multiple_of(j * width, width), width)
        dot[...] = jnp.dot(left[...], dots_ref[:, chunk], preferred_element_type=F32)
        for i in range(count // rows):
            here = slice(i * rows, (i + 1) * rows)
            active = [
                jnp.concatenate([spread[c, here, :]] * (lanes // LANES), axis=1)
                for c in range(3)
            ]
            for l in range(width // lanes):
                there = slice(l * lanes, (l + 1) * lanes)
                block = j * (width // block_width) + l * lanes // block_width
                start = l * lanes % block_width
                offset = [
                    slab_ref[block, c:c + 1, start:start + lanes] - active[c] for c in range(3)
                ]
                distance_sq = offset[0] * offset[0] + (
                    offset[1] * offset[1] + (offset[2] * offset[2] + SOFTEN_SQ)
                )
                inverse = lax.rsqrt(distance_sq)
                inverse_sq = inverse * inverse
                weight = inverse * inverse_sq
                rate = weight * (dot[here, there] * inverse_sq)
                for n, value in enumerate((weight, rate)):
                    high = value.astype(BF16)
                    low = (value - high.astype(F32)).astype(BF16)
                    at = 2 * n * count + i * rows
                    terms[at:at + rows, there] = high
                    terms[at + count:at + count + rows, there] = low
        total[...] += lax.dot_general(
            terms[...], sums_ref[:, chunk], (((1,), (1,)), ((), ())), preferred_element_type=F32
        )
        return 0

    lax.fori_loop(0, blocks * block_width // width, step, 0)
    sums = total[0:2 * count, :].reshape(2, count, 32)
    rates = total[2 * count:4 * count, :].reshape(2, count, 32)
    sums = jnp.transpose(sums[0] + sums[1])
    rates = jnp.transpose(rates[0] + rates[1])
    sums = sums[0:8, :] + sums[8:16, :] + sums[16:24, :]
    rates = rates[0:8, :] + rates[8:16, :] + rates[16:24, :]
    accel = sums[0:3, :] - position * sums[6:7, :]
    jerk = sums[3:6, :] - velocity * sums[6:7, :]
    jerk = jerk - 3.0 * (rates[0:3, :] - position * rates[6:7, :])
    out_ref[...] = jnp.concatenate([accel, jerk, jnp.zeros((2, count), F32)], axis=0)


def call(kernel, outs, scratch=(), name=None):
    return pl.pallas_call(
        kernel,
        out_shape=outs,
        scratch_shapes=list(scratch),
        compiler_params=pltpu.CompilerParams(vmem_limit_bytes=40 * 2**20),
        name=name,
    )


def spread_over(value, axes):
    size = lax.axis_size(axes)
    return lax.all_to_all(jnp.broadcast_to(value[None], (size,) + value.shape), axes, 0, 0)


def local(phase, masses, active_index):
    width = phase.shape[1]
    count = active_index.shape[0]
    rows_count, cols_count = lax.axis_size(ROW), lax.axis_size(COL)
    stars = width * rows_count * cols_count
    core = lax.axis_index("c")
    half = spread_over(jnp.concatenate([phase, masses, jnp.zeros_like(masses)], axis=0), ("yl", "z"))
    other = lax.ppermute(half, "c", [(0, 1), (1, 0)])
    slab = jnp.concatenate([half, other], axis=0)

    slab_width = width * cols_count
    block = active_index // width
    column = block % cols_count
    place = (column % 2 != core) * (cols_count // 2) + column // 2
    place = jnp.where(active_index // slab_width == lax.axis_index(ROW), place, -1)
    where = jnp.stack([place, active_index % width])

    picked = call(pick_kernel, jax.ShapeDtypeStruct((8, count), F32), name="pick")(slab, where)
    picks = spread_over(picked, ROW)
    sums, dots, centre = call(
        field_kernel,
        (
            jax.ShapeDtypeStruct((32, slab_width), BF16),
            jax.ShapeDtypeStruct((48, slab_width), BF16),
            jax.ShapeDtypeStruct((8, LANES), F32),
        ),
        name="field",
    )(slab)
    chunk = 1024
    partial = call(
        functools.partial(pair_kernel, width=chunk, rows=16, lanes=256),
        jax.ShapeDtypeStruct((8, count), F32),
        (
            pltpu.VMEM((3, count, LANES), F32),
            pltpu.VMEM((count, 48), BF16),
            pltpu.VMEM((count, chunk), F32),
            pltpu.VMEM((4 * count, chunk), BF16),
            pltpu.VMEM((4 * count, 32), F32),
        ),
        name="pairs",
    )(slab, sums, dots, centre, picks)
    total = jnp.sum(spread_over(partial[0:6], ROW), axis=0) * (1.0 / stars)
    return total[0:3], total[3:6]


def solution(mesh):
    fine = Mesh(mesh.devices.reshape(4, 4, 2, 8, 2), NAMES)
    stars = P(None, ROW + COL)
    return jax.shard_map(
        local,
        mesh=fine,
        in_specs=(stars, stars, P(COL)),
        out_specs=(P(None, COL), P(None, COL)),
        check_vma=False,
    )
```

```python
import jax
import jax.numpy as jnp
from jax import lax
from jax.experimental import pallas as pl
from jax.experimental.pallas import tpu as pltpu
from jax.sharding import Mesh, PartitionSpec as P

SOFTEN_SQ = 0.0001
NAMES = ("x", "yh", "yl", "z", "c")
ROW = ("x", "yh")
COL = ("yl", "z", "c")
LANES = 128
TILE = 256
STEP = 16
SPAN = 32
SPANS = LANES // SPAN
GROUPS = 2
SLOTS = 2
COARSE = 1.5 * 2.0**19
MIDDLE = 1.5 * 2.0**11
F32 = jnp.float32
BF16 = jnp.bfloat16
HBM = pl.BlockSpec(memory_space=pltpu.HBM)
VMEM = pl.BlockSpec(memory_space=pltpu.VMEM)


def pieces(value):
    high = value.astype(BF16)
    rest = value - high.astype(F32)
    middle = rest.astype(BF16)
    low = (rest - middle.astype(F32)).astype(BF16)
    return high, middle, low


def copies_kernel(phase_ref, masses_ref, out_ref, block, sems):
    loads = [
        pltpu.make_async_copy(phase_ref, block.at[0:6, :], sems.at[0]),
        pltpu.make_async_copy(masses_ref, block.at[6:7, :], sems.at[1]),
    ]
    for load in loads:
        load.start()
    block[7:8, :] = jnp.zeros((1, block.shape[1]), F32)
    for load in loads:
        load.wait()
    for n in range(out_ref.shape[0]):
        out_ref[n] = block[...]


def pick_kernel(
    half_ref, other_ref, index_hbm, picks_ref, own_ref, hits_ref, index_ref, sem
):
    blocks, _, width = half_ref.shape
    count = index_ref.shape[1]
    load = pltpu.make_async_copy(index_hbm, index_ref, sem.at[0])
    load.start()
    values = []
    for c in range(7):
        both = jnp.concatenate([half_ref[:, c, :], other_ref[:, c, :]], axis=0)
        values.append(jnp.concatenate(pieces(both), axis=0))
    load.wait()
    index = index_ref[...]
    column = index // width
    place = index - column * width
    row = column // (2 * blocks)
    column = column - row * (2 * blocks)
    block = column // 2
    block = jnp.where(column - 2 * block == lax.axis_index("c"), block, block + blocks)
    here_row = lax.axis_index("x") * lax.axis_size("yh") + lax.axis_index("yh")
    block = jnp.where(row == here_row, block, -1)
    one_hot = lax.broadcasted_iota(jnp.int32, (2 * blocks, count), 0) == block
    one_hot = jnp.where(one_hot, 1.0, 0.0).astype(BF16)
    three = jnp.concatenate([one_hot, one_hot, one_hot], axis=0)
    here = lax.broadcasted_iota(jnp.int32, (width, count), 0) == place
    rows = []
    for c in range(7):
        taken = lax.dot_general(
            values[c], three, (((0,), (0,)), ((), ())), preferred_element_type=F32
        )
        rows.append(jnp.sum(jnp.where(here, taken, 0.0), axis=0, keepdims=True))
    zero = jnp.zeros((1, count), F32)
    own_ref[...] = jnp.concatenate(rows + [zero], axis=0)
    state = jnp.concatenate(rows[0:6], axis=0)
    for n in range(picks_ref.shape[0]):
        picks_ref[n] = state
    here = jnp.where(here, 1.0, 0.0).astype(BF16)
    hits_ref[...] = lax.dot_general(
        one_hot, here, (((1,), (1,)), ((), ())), preferred_element_type=F32
    )


def levels(position):
    coarse = (position + COARSE) - COARSE
    rest = position - coarse
    middle = (rest + MIDDLE) - MIDDLE
    return coarse, middle, (rest - middle).astype(BF16).astype(F32)


def squares(coarse, middle, fine):
    rest = middle + fine
    first = jnp.sum(coarse * coarse, axis=0, keepdims=True)
    second = 2.0 * jnp.sum(coarse * middle, axis=0, keepdims=True)
    third = jnp.sum(rest * rest + 2.0 * coarse * fine, axis=0, keepdims=True)
    return first, second, third


def wide(parts):
    return [part.astype(F32) for part in parts]


def field_kernel(half_ref, other_ref, own_ref, hits_ref, dots_ref, near_ref, sums_ref, centre_ref):
    blocks, _, width = half_ref.shape
    total = jnp.zeros((8, width), F32)
    for b in range(blocks):
        total = total + (half_ref[b] + other_ref[b])
    mean = jnp.sum(total, axis=1, keepdims=True) * (1.0 / (2 * blocks * width))
    centre = jnp.where(lax.broadcasted_iota(jnp.int32, (8, 1), 0) < 6, mean, 0.0)
    centre_ref[...] = jnp.broadcast_to(centre, (8, LANES))

    def block_terms(raw, mass, at):
        size = raw.shape[1]
        rows = lax.broadcasted_iota(jnp.int32, (8, size), 0)
        star = raw - centre
        where = pl.ds(pl.multiple_of(at, size), size)
        sums_ref[:, where] = jnp.where(rows == 6, mass, star * mass)
        along = jnp.sum(star[0:3, :] * star[3:6, :], axis=0, keepdims=True)
        terms = jnp.where(rows == 6, along, star)
        terms = jnp.where(rows == 7, 1.0, terms)
        high, middle, low = wide(pieces(terms))
        dot = jnp.concatenate([high, middle, low, high], axis=0)
        coarse, middle, fine = levels(raw[0:3, :])
        first, second, third = squares(coarse, middle, fine)
        first, second = wide(pieces(first)), wide(pieces(second))
        third = wide(pieces(third + SOFTEN_SQ))
        one, zero = jnp.ones_like(mass), jnp.zeros((3, size), F32)
        near = [coarse, one, first[0], first[1], second[0], second[1]]
        near += [middle, one, middle, one, fine, one]
        near += [coarse, third[0], fine, third[1], third[2], zero]
        near = jnp.concatenate(near, axis=0)
        cuts = [slice(n, n + TILE) for n in range(0, size, TILE)]
        return [dot[:, cut] for cut in cuts], [near[:, cut] for cut in cuts]

    def left(spans):
        spans = spans + [jnp.zeros_like(spans[0])] * (SPANS - len(spans))
        return jnp.transpose(jnp.concatenate(spans, axis=0)).astype(BF16)

    per = SPANS * TILE // width

    def step(i, _):
        for side, ref in enumerate((half_ref, other_ref)):
            at = i + side * (blocks // per)
            dots, nears = [], []
            for k in range(per):
                raw = ref[i * per + k]
                n = at * per + k
                mass = raw[6:7, :] * (1.0 - hits_ref[pl.ds(n, 1), :])
                dot, near = block_terms(raw, mass, n * width)
                dots += dot
                nears += near
            dots_ref[at] = left(dots)
            near_ref[at] = left(nears)
        return 0

    lax.fori_loop(0, blocks // per, step, 0)
    own = own_ref[...]
    dots, nears = block_terms(own, own[6:7, :], 2 * blocks * width)
    dots_ref[dots_ref.shape[0] - 1] = left(dots)
    near_ref[near_ref.shape[0] - 1] = left(nears)


def pair_kernel(dots_ref, near_ref, sums_ref, centre_ref, picks_ref, out_ref, dot_right, near_right, parts):
    count = picks_ref.shape[2]
    groups = dots_ref.shape[0] - 1
    state = picks_ref[0]
    for n in range(1, picks_ref.shape[0]):
        state = state + picks_ref[n]
    local = state - centre_ref[0:6, 0:1]
    position, velocity = local[0:3, :], local[3:6, :]
    along = jnp.sum(position * velocity, axis=0, keepdims=True)
    one, zero = jnp.ones((1, count), F32), jnp.zeros((1, count), F32)
    high, middle, low = wide(
        pieces(jnp.concatenate([-velocity, -position, one, along], axis=0))
    )
    none = jnp.zeros_like(high)
    dot_rows = (
        jnp.concatenate([high, high, high, middle], axis=0),
        jnp.concatenate([low, middle, none, none], axis=0),
    )
    split = levels(state[0:3, :])
    first, second, third = (wide(pieces(part)) for part in squares(*split))
    coarse, middle, fine = (-2.0 * part for part in split)
    none = jnp.zeros((3, count), F32)
    near_rows = (
        jnp.concatenate(
            [coarse, first[0], one, one, one, one, coarse, second[0], middle, third[0]]
            + [middle, third[2], fine, one, coarse, one, one, none],
            axis=0,
        ),
        jnp.concatenate(
            [middle, first[1], zero, none, none, second[1], fine, third[1], fine, zero]
            + [zero, none] * 3,
            axis=0,
        ),
    )
    for right, (rows, more) in ((dot_right, dot_rows), (near_right, near_rows)):
        none = jnp.zeros_like(rows)
        for n in range(SPANS):
            both = [rows if m == n else none for m in range(SPANS)]
            both += [more if m == n else none for m in range(SPANS)]
            right[n] = jnp.concatenate(both, axis=0).astype(BF16)

    steps = TILE // STEP

    def sums_of(total_w, total_r, dots, nears):
        planes = ((near_ref, near_right, 1, nears), (dots_ref, dot_right, 0, dots))

        def stage(tile):
            for _, right, m, _ in planes:
                pltpu.matmul_push_rhs(right[tile % SPANS], 0, m)

        def product(group, tile, t):
            block = group + tile // SPANS
            for left_ref, _, _, results in planes:
                rows = left_ref[block, t * STEP:(t + 1) * STEP, :]
                pltpu.matmul_acc_lhs(
                    results[tile % SLOTS][t],
                    jnp.concatenate([rows, rows], axis=1),
                    load_staged_rhs=0 if t == 0 else None,
                )

        def pairs(tile, t, masked):
            inverse = lax.rsqrt(pltpu.matmul_pop(nears[tile % SLOTS][t]))
            inverse_sq = inverse * inverse
            weight = inverse * inverse_sq
            if masked:
                star = lax.broadcasted_iota(jnp.int32, (STEP, TILE), 0) + t * STEP
                active_star = lax.broadcasted_iota(jnp.int32, (STEP, TILE), 1)
                weight = jnp.where(star == active_star, 0.0, weight)
            rate = weight * (pltpu.matmul_pop(dots[tile % SLOTS][t]) * inverse_sq)
            rows = slice(t * STEP, (t + 1) * STEP)
            for m, value in enumerate((weight, rate)):
                high = value.astype(BF16)
                parts[tile % 2, m, 0, rows, :] = high
                parts[tile % 2, m, 1, rows, :] = (value - high.astype(F32)).astype(BF16)

        def stage_parts(tile):
            for n in range(2):
                for m in range(2):
                    pltpu.matmul_push_rhs(parts[tile % 2, m, n], 1 - n, m)

        def add(number):
            start = pl.multiple_of(jnp.maximum(number, 0) * TILE, TILE)
            field = pieces(sums_ref[:, pl.ds(start, TILE)])
            field = jnp.concatenate(field + (jnp.zeros_like(field[0]),), axis=0)
            for n in range(2):
                for m, total in enumerate((total_w, total_r)):
                    pltpu.matmul_acc_lhs(total, field, load_staged_rhs=1 - n)

        parts[1] = jnp.zeros_like(parts[1])
        stage(0)
        for t in range(steps):
            product(0, 0, t)
        stage(1)
        tiles = GROUPS * SPANS

        def step(i, _):
            for tile in range(tiles):
                product(i * GROUPS, tile + 1, 0)
                stage_parts(tile + 1)
                pairs(tile, 0, False)
                for t in range(1, steps):
                    product(i * GROUPS, tile + 1, t)
                    pairs(tile, t, False)
                add(i * tiles + tile - 1)
                stage(tile + 2)
            return 0

        lax.fori_loop(0, groups // GROUPS, step, 0)
        product(groups, 1, 0)
        for results in (nears, dots):
            pltpu.matmul_pop(results[1 % SLOTS][0])
        stage_parts(1)
        for t in range(steps):
            pairs(0, t, True)
        add(groups * SPANS - 1)
        stage_parts(0)
        add(groups * SPANS)
        sums = pltpu.matmul_pop(total_w)
        rates = pltpu.matmul_pop(total_r)
        sums = sums[0:8, :] + sums[8:16, :] + sums[16:24, :]
        rates = rates[0:8, :] + rates[8:16, :] + rates[16:24, :]
        accel = sums[0:3, :] - position * sums[6:7, :]
        jerk = sums[3:6, :] - velocity * sums[6:7, :]
        jerk = jerk - 3.0 * (rates[0:3, :] - position * rates[6:7, :])
        both = jnp.concatenate([accel, jerk], axis=0)
        for n in range(out_ref.shape[0]):
            out_ref[n] = both

    def results(m):
        return [[pltpu.ACC(m)((STEP, TILE), F32) for _ in range(steps)] for _ in range(SLOTS)]

    pl.run_scoped(
        sums_of,
        pltpu.ACC(0)((32, TILE), F32),
        pltpu.ACC(1)((32, TILE), F32),
        results(0),
        results(1),
    )


def call(kernel, name, outs, scratch=(), ins=None):
    more = {} if ins is None else {"in_specs": ins}
    return pl.pallas_call(
        kernel,
        out_shape=outs,
        **more,
        scratch_shapes=list(scratch),
        compiler_params=pltpu.CompilerParams(vmem_limit_bytes=40 * 2**20),
        name=name,
    )


def shape(*sizes, dtype=F32):
    return jax.ShapeDtypeStruct(sizes, dtype)


def local(phase, masses, active_index):
    width = phase.shape[1]
    count = active_index.shape[0]
    rows_count, cols_count = lax.axis_size(ROW), lax.axis_size(COL)
    stars = width * rows_count * cols_count
    near = ("yl", "z")
    near_count = lax.axis_size(near)

    copies = call(
        copies_kernel,
        "copies",
        shape(near_count, 8, width),
        (pltpu.VMEM((8, width), F32), pltpu.SemaphoreType.DMA((2,))),
        [HBM, HBM],
    )(phase, masses)
    half = lax.all_to_all(copies, near, 0, 0)
    other = lax.ppermute(half, "c", [(0, 1), (1, 0)])
    picks, own, hits = call(
        pick_kernel,
        "pick",
        (shape(rows_count, 6, count), shape(8, count), shape(cols_count, width)),
        (pltpu.VMEM((1, count), jnp.int32), pltpu.SemaphoreType.DMA((1,))),
        [VMEM, VMEM, HBM],
    )(half, other, active_index.reshape(1, count))
    picks = lax.all_to_all(picks, ROW, 0, 0)
    factor = shape(cols_count * width // (TILE * SPANS) + 1, TILE, LANES, dtype=BF16)
    dots, near, sums, centre = call(
        field_kernel,
        "field",
        (factor, factor, shape(8, cols_count * width + count), shape(8, LANES)),
    )(half, other, own, hits)
    right = pltpu.VMEM((SPANS, TILE, count), BF16)
    parts = pltpu.VMEM((2, 2, 2, TILE, count), BF16)
    partial = call(pair_kernel, "pairs", shape(rows_count, 6, count), (right, right, parts))(
        dots, near, sums, centre, picks
    )
    total = jnp.sum(lax.all_to_all(partial, ROW, 0, 0), axis=0) * (1.0 / stars)
    return total[0:3], total[3:6]


def solution(mesh):
    fine = Mesh(mesh.devices.reshape(4, 4, 2, 8, 2), NAMES)
    stars = P(None, ROW + COL)
    return jax.shard_map(
        local,
        mesh=fine,
        in_specs=(stars, stars, P(COL)),
        out_specs=(P(None, COL), P(None, COL)),
        check_vma=False,
    )
```
